512 devices in a mesh: head: 8 (over x, core), outer: 16 (over y_hi, z), inner: 4 (over y_lo).
Axes of the slice: x: 4, y: 8 (y_hi: 2, y_lo: 4; y = y_hi * 4 + y_lo), z: 8, core: 2. Of those that a mesh axis runs over, the one named last changes fastest.
Arguments:
- queries: bfloat16 [8192, 24, 128], P(('outer', 'inner'), 'head'), may hold values from -9 to 9
- key_states: bfloat16 [64, 8, 16, 8, 128], P(('outer', 'inner'), 'head'), may hold values from -5 to 5
- value_states: bfloat16 [64, 8, 16, 8, 128], P(('outer', 'inner'), 'head'), may hold values from -6 to 6
- head_masks: int32 [24, 128, 128], P('head'), may hold values from 0 to 1, as said below
Outputs:
- attended: bfloat16 [8192, 24, 128], P(('outer', 'inner'), 'head')
The draws below stay inside these ranges and needn't reach their ends.
Inputs may be any that keep to these rules, and one draw needn't show every extreme that they name: head_masks[h, i, j] is 0 for j > i and 1 for j = i and j = i - 1; other entries below the diagonal are 1 at a rate that differs by head.
All inputs are finite; a program needn't handle non-finite values.
Results may differ from the reference program's by a relative error of at most 0.0045.
Values may be sent and summed in bfloat16 or wider, within the bound.
No kernel may reach another device: no remote copies, remote signals or barrier semaphores. Data moves between devices by JAX's collectives and lax.ppermute only.
A program may use at most 128 MiB of HBM per device.

```python
import jax
import jax.numpy as jnp
from jax import lax

HD = 128
KVH = 8
GROUP = 3
NB = 128
QH = 24
SHARDS = 64
SUBS = 8
SUBROWS = 16
TOKENS = 8192
BLK = 64


def draw_queries(key, part):
    key = jax.random.fold_in(key, 1)
    drawn_draw = 3.0 * jax.random.truncated_normal(key, -3.0, 3.0, (TOKENS, QH, HD), jnp.float32)
    return drawn_draw.astype(jnp.bfloat16)


def draw_key_states(key, part):
    key = jax.random.fold_in(key, 2)
    drawn_draw = jax.random.truncated_normal(key, -5.0, 5.0, (TOKENS, KVH, HD), jnp.float32)
    return drawn_draw.reshape(SHARDS, SUBS, SUBROWS, KVH, HD).astype(jnp.bfloat16)


def draw_head_masks(key, part):
    key = jax.random.fold_in(key, 5)
    rate_key, roll_key = jax.random.split(key)
    edge_rate = jax.random.randint(rate_key, (QH, 1, 1), 20, 600)
    edge_roll = jax.random.randint(roll_key, (QH, NB, NB), 0, 1000)
    row_block = jnp.arange(NB, dtype=jnp.int32)[:, None]
    col_block = jnp.arange(NB, dtype=jnp.int32)[None, :]
    near_band = (col_block <= row_block) & (col_block >= row_block - 1)
    below_diag = col_block < row_block
    chosen = near_band[None] | below_diag[None] & (edge_roll < edge_rate)
    return chosen.astype(jnp.int32)


def block_scale(rng, dims, cuts, smallest, largest):
    gain, own = 1.0, jax.random.fold_in(rng, 6)
    for position, blocks in cuts:
        draws = jnp.exp(jax.random.uniform(jax.random.fold_in(own, position), (blocks,), jnp.float32, smallest / len(cuts), largest / len(cuts)))
        gain = gain * jnp.repeat(draws, dims[position] // blocks).reshape([-1 if axis == position else 1 for axis in range(len(dims))])
    return gain


def scatter_about(key, extent, scale, reach, shards=(), kind=jnp.bfloat16):
    level = block_scale(key, extent, shards, -0.22, 0.18) if shards else 1.0
    result = jax.random.normal(key, extent, jnp.float32) * scale * level
    return jnp.minimum(jnp.maximum(result, -reach), reach).astype(kind)


def setup_inputs(seed: int = 0) -> dict:
    streams_of = jax.random.split(jax.random.key(seed), 5)
    queries = draw_queries(jax.random.fold_in(streams_of[4], 71), 0)
    key_states = draw_key_states(jax.random.fold_in(streams_of[4], 71), 0)
    value_states = scatter_about(streams_of[2], (SHARDS, SUBS, SUBROWS, KVH, HD), 1.0, 6.0, ((0, 64), (1, 8)))
    head_masks = draw_head_masks(jax.random.fold_in(streams_of[4], 71), 0)
    return dict(queries=queries, key_states=key_states, value_states=value_states, head_masks=head_masks)


def reference(queries, key_states, value_states, head_masks):
    key_flat = key_states.reshape(TOKENS, KVH, HD)
    value_flat = value_states.reshape(TOKENS, KVH, HD)
    block_rows = min(512, TOKENS)
    key_index = jnp.arange(TOKENS, dtype=jnp.int32)
    score_scale = HD ** -0.5

    def one_block(block_index):
        first_row = block_index * block_rows
        query_block = lax.dynamic_slice_in_dim(queries, first_row, block_rows, 0)
        query_index = first_row + jnp.arange(block_rows, dtype=jnp.int32)
        mask_rows = jnp.take(head_masks, query_index // BLK, axis=1)
        causal = query_index[:, None] >= key_index[None, :]

        def one_head(kv_head):
            query_group = lax.dynamic_slice_in_dim(query_block, kv_head * GROUP, GROUP, 1).astype(jnp.float32)
            key_head = lax.dynamic_index_in_dim(key_flat, kv_head, 1, keepdims=False).astype(jnp.float32)
            value_head = lax.dynamic_index_in_dim(value_flat, kv_head, 1, keepdims=False).astype(jnp.float32)
            scores = jnp.einsum("qgd,cd->gqc", query_group, key_head) * score_scale
            mask_group = lax.dynamic_slice_in_dim(mask_rows, kv_head * GROUP, GROUP, 0)
            allowed = (jnp.repeat(mask_group, BLK, axis=2) > 0) & causal[None]
            masked = jnp.where(allowed, scores, -1e30)
            highest = jnp.max(masked, axis=2, keepdims=True)
            weights = jnp.exp(masked - highest)
            denominator = jnp.sum(weights, axis=2)
            rounded = lax.optimization_barrier(weights.astype(jnp.bfloat16)).astype(jnp.float32)
            weighted = jnp.einsum("gqc,cd->gqd", rounded, value_head)
            return (weighted / denominator[:, :, None]).astype(jnp.bfloat16)

        per_head = lax.map(one_head, jnp.arange(KVH, dtype=jnp.int32))
        return per_head.reshape(QH, block_rows, HD).transpose(1, 0, 2)

    blocks = lax.map(one_block, jnp.arange(TOKENS // block_rows, dtype=jnp.int32))
    return blocks.reshape(TOKENS, QH, HD)
```

```python
import jax
import jax.numpy as jnp
from jax import lax
from jax.experimental import pallas as pl
from jax.experimental.pallas import tpu as pltpu
from jax.sharding import Mesh, PartitionSpec as P

HEAD = ("x", "c")
KEYS = ("yh", "zs", "ys")
BLOCK = ("z0", "y0")
TOK = ("yh", "zs", "z0", "ys", "y0")
AXES = HEAD + TOK
SIZES = (4, 2, 2, 4, 2, 2, 2)

HD = 128
ROWS = 128
GROUP = 3
QROWS = GROUP * ROWS
BLK = 64
MASKED = -1e30
LOG2E = 1.4426950408889634
SCALE2 = HD**-0.5 * LOG2E


def attend_kernel(place_ref, q_ref, kv_ref, mask_ref, out_ref, kx_ref, vx_ref, s_ref):
    shards = kv_ref.shape[1]
    own = place_ref[0]
    lane = lax.broadcasted_iota(jnp.int32, (ROWS, HD), 1)
    row = lax.broadcasted_iota(jnp.int32, (ROWS, HD), 0)
    row_half = row // BLK
    for s in range(shards):
        rows = pl.ds(s * ROWS, ROWS)
        kx_ref[rows, :HD] = kv_ref[:, s, 0].reshape(ROWS, HD)
        vx_ref[rows, :HD] = kv_ref[:, s, 1].reshape(ROWS, HD)
        block = 2 * place_ref[8 + s] + row_half
        kx_ref[rows, HD:] = jnp.where(lane == block, 1.0, 0.0).astype(jnp.bfloat16)
        vx_ref[rows, HD:] = jnp.ones((ROWS, HD), jnp.bfloat16)

    def one_shard(j, carry):
        shard = place_ref[1 + j]
        biases = []
        for g in range(GROUP):
            for half in range(2):
                mask = mask_ref[g, pl.ds(2 * shard + half, 1), :]
                bias = jnp.where(mask > 0, 0.0, MASKED)
                biases.append(jnp.broadcast_to(bias, (BLK, HD)).astype(jnp.bfloat16))
        qx = jnp.concatenate([q_ref[j].reshape(QROWS, HD), jnp.concatenate(biases, axis=0)], axis=1)
        s_ref[...] = lax.dot_general(
            qx, kx_ref[...], (((1,), (1,)), ((), ())), preferred_element_type=jnp.float32
        )

        @pl.when(j == 0)
        def _():
            cols = pl.ds(pl.multiple_of(own * ROWS, ROWS), ROWS)
            for g in range(GROUP):
                rows = pl.ds(g * ROWS, ROWS)
                s_ref[rows, cols] = jnp.where(lane <= row, s_ref[rows, cols], MASKED)

        stats = []
        for g in range(GROUP):
            rows = pl.ds(g * ROWS, ROWS)
            scores = s_ref[rows, :]
            highest = jnp.max(scores, axis=1, keepdims=True)
            weights = jnp.exp2((scores - highest) * SCALE2).astype(jnp.bfloat16)
            both = jnp.dot(weights, vx_ref[...], preferred_element_type=jnp.float32)
            denominator = both[:, HD:]
            out_ref[j, rows, :] = (both[:, :HD] / denominator).astype(jnp.bfloat16)
            stats.append(highest * SCALE2 + jnp.log2(denominator))
        which = lane % GROUP
        level = jnp.where(which == 0, stats[0], jnp.where(which == 1, stats[1], stats[2]))
        high = level.astype(jnp.bfloat16).astype(jnp.float32)
        rest = level - high
        middle = rest.astype(jnp.bfloat16).astype(jnp.float32)
        parts = jnp.where(lane < GROUP, high, jnp.where(lane < 2 * GROUP, middle, rest - middle))
        out_ref[j, pl.ds(QROWS, 16), :] = parts.T[:16].astype(jnp.bfloat16)
        return carry

    lax.fori_loop(0, q_ref.shape[0], one_shard, 0)


def combine_kernel(p_ref, out_ref):
    parts = p_ref.shape[0]
    levels = []
    for i in range(parts):
        st = p_ref[i, pl.ds(QROWS, 16), :].astype(jnp.float32)
        levels.append(st[0:GROUP] + st[GROUP : 2 * GROUP] + st[2 * GROUP : 3 * GROUP])
    top = levels[0]
    for i in range(1, parts):
        top = jnp.maximum(top, levels[i])
    shares = [jnp.exp2(level - top) for level in levels]
    total = shares[0]
    for i in range(1, parts):
        total = total + shares[i]
    shares = [share / total for share in shares]
    pad = jnp.zeros((HD - parts * GROUP, HD), jnp.float32)
    columns = jnp.concatenate(shares + [pad], axis=0).T
    for g in range(GROUP):
        acc = None
        for i in range(parts):
            c = i * GROUP + g
            term = p_ref[i, pl.ds(g * ROWS, ROWS), :].astype(jnp.float32) * columns[:, c : c + 1]
            acc = term if acc is None else acc + term
        out_ref[g] = acc.astype(jnp.bfloat16)


def swap(value, axis):
    return lax.ppermute(value, axis, [(0, 1), (1, 0)])


def per_device(queries, key_states, value_states, head_masks):
    yh, zs, z0, ys, y0 = (lax.axis_index(a) for a in TOK)
    shard_of = lambda yh, zs, z0, ys, y0: yh * 32 + zs * 8 + z0 * 4 + ys * 2 + y0

    mine = queries.transpose(1, 0, 2)
    pair = jnp.stack([mine, swap(mine, "y0")])
    other = swap(pair, "z0")
    q_all = jnp.concatenate([pair, other], axis=0)
    q_shards = [shard_of(yh, zs, z0 ^ (j >> 1), ys, y0 ^ (j & 1)) for j in range(4)]

    kv = jnp.stack([key_states[0, 0], value_states[0, 0]]).transpose(2, 0, 1, 3)
    kv = jnp.broadcast_to(kv[:, None], (8, 16, 2, 16, HD)).reshape(128, 2, 16, HD)
    kv = lax.all_to_all(kv, HEAD + KEYS, 0, 0, tiled=True).reshape(8, 16, 2, 16, HD)
    k_shards = [shard_of(i >> 3, (i >> 1) & 3, z0, i & 1, y0) for i in range(16)]
    own = yh * 8 + zs * 2 + ys

    place = jnp.stack(
        [own] + q_shards + [jnp.int32(0)] * 3 + k_shards
    ).astype(jnp.int32)
    vmem = pl.BlockSpec(memory_space=pltpu.VMEM)
    parts = pl.pallas_call(
        attend_kernel,
        out_shape=jax.ShapeDtypeStruct((4, QROWS + 16, HD), jnp.bfloat16),
        in_specs=[pl.BlockSpec(memory_space=pltpu.SMEM), vmem, vmem, vmem],
        out_specs=vmem,
        scratch_shapes=[
            pltpu.VMEM((16 * ROWS, 2 * HD), jnp.bfloat16),
            pltpu.VMEM((16 * ROWS, 2 * HD), jnp.bfloat16),
            pltpu.VMEM((QROWS, 16 * ROWS), jnp.float32),
        ],
        compiler_params=pltpu.CompilerParams(vmem_limit_bytes=32 * 2**20),
        name="attend",
    )(place, q_all, kv, head_masks)

    got = [parts[0]] + [
        lax.ppermute(parts[j], BLOCK, [(i, i ^ j) for i in range(4)]) for j in (3, 2, 1)
    ]
    got = jnp.stack(got)
    out = pl.pallas_call(
        combine_kernel,
        out_shape=jax.ShapeDtypeStruct((GROUP, ROWS, HD), jnp.bfloat16),
        in_specs=[vmem],
        out_specs=vmem,
        compiler_params=pltpu.CompilerParams(vmem_limit_bytes=16 * 2**20),
        name="combine",
    )(got)
    return out.transpose(1, 0, 2)


def solution(mesh):
    fine = Mesh(mesh.devices.reshape(SIZES), AXES)
    return jax.shard_map(
        per_device,
        mesh=fine,
        in_specs=(P(TOK, HEAD, None), P(TOK, HEAD), P(TOK, HEAD), P(HEAD)),
        out_specs=P(TOK, HEAD, None),
        check_vma=False,
    )
```

```python
import functools

import jax
import jax.numpy as jnp
from jax import lax
from jax.experimental import pallas as pl
from jax.experimental.pallas import tpu as pltpu
from jax.sharding import Mesh, PartitionSpec as P

HEAD = ("x", "c")
TOK = ("yh", "zs", "z0", "ys", "y0")
BLOCK = ("z0", "y0")
AXES = HEAD + TOK
PLANE = ("c",) + TOK
SIZES = (4, 2, 2, 4, 2, 2, 2)

HD = 128
ROWS = 128
GROUP = 3
QROWS = GROUP * ROWS
STAT = 16
BLK = 64
FAR = 4
MASKED = -1e30
LOG2E = 1.4426950408889634
SCALE2 = HD**-0.5 * LOG2E


def plane_index(c, y, z):
    return c * 64 + (y >> 2) * 32 + z * 4 + (y & 3)


def plane_places():
    return [(c, y, z) for c in range(2) for y in range(8) for z in range(8)]


def second_axis_shift(r):
    pairs = []
    for c, y, z in plane_places():
        to = ((y + 2 * r) % 8, z) if c == 0 else (y, (z + 2 * r) % 8)
        pairs.append((plane_index(c, y, z), plane_index(c, *to)))
    return pairs


def first_axis_groups():
    groups = {}
    for x in range(4):
        for c, y, z in plane_places():
            key = (c, y, z & 1) if c == 0 else (c, y & 1, z)
            groups.setdefault(key, []).append(x * 128 + plane_index(c, y, z))
    return list(groups.values())


def shard_of(y, z):
    return (y >> 2) * 32 + z * 4 + (y & 3)


def attend_kernel(first, last, chunks, place_ref, qa_ref, qb_ref, mask_ref, *refs):
    kv_refs, refs = refs[:chunks], refs[chunks:]
    if not first:
        acc_in, top_in, den_in, refs = refs[0], refs[1], refs[2], refs[3:]
    if last:
        out_ref, refs = refs[0], refs[1:]
    else:
        acc_out, top_out, den_out, refs = refs[0], refs[1], refs[2], refs[3:]
    qx_ref, kx_ref, vx_ref, s_ref = refs
    base = 8 + (0 if first else (4 - chunks) * FAR)
    lane = lax.broadcasted_iota(jnp.int32, (ROWS, HD), 1)
    row = lax.broadcasted_iota(jnp.int32, (ROWS, HD), 0)
    row_half = row // BLK
    for n, kv_ref in enumerate(kv_refs):
        for k in range(FAR):
            s = n * FAR + k
            rows = pl.ds(s * ROWS, ROWS)
            kx_ref[:HD, rows] = kv_ref[:, k, :, 0].reshape(ROWS, HD).T
            vx_ref[rows, :HD] = kv_ref[:, k, :, 1].reshape(ROWS, HD)
            block = 2 * place_ref[base + s] + lane // BLK
            kx_ref[HD:, rows] = jnp.where(row == block, 1.0, 0.0).astype(jnp.bfloat16)
            vx_ref[rows, HD:] = jnp.ones((ROWS, HD), jnp.bfloat16)
    for j in range(4):
        src = (qa_ref, qb_ref)[j >> 1]
        shard = place_ref[1 + j]
        qx_ref[j, :, :HD] = src[j & 1].reshape(QROWS, HD)
        for g in range(GROUP):
            for half in range(2):
                bias = jnp.where(mask_ref[g, pl.ds(2 * shard + half, 1), :] > 0, 0.0, MASKED)
                rows = pl.ds(g * ROWS + half * BLK, BLK)
                qx_ref[j, rows, HD:] = jnp.broadcast_to(bias, (BLK, HD)).astype(jnp.bfloat16)

    def one_shard(j, carry):
        s_ref[j] = jnp.dot(qx_ref[j], kx_ref[...], preferred_element_type=jnp.float32)
        if first and j == 0:
            cols = pl.ds(pl.multiple_of(place_ref[0] * ROWS, ROWS), ROWS)
            for g in range(GROUP):
                rows = pl.ds(g * ROWS, ROWS)
                s_ref[j, rows, cols] = jnp.where(lane <= row, s_ref[j, rows, cols], MASKED)

        stats = []
        for g in range(GROUP):
            rows = pl.ds(g * ROWS, ROWS)
            scores = s_ref[j, rows, :]
            highest = jnp.max(scores, axis=1, keepdims=True)
            if not first:
                before = top_in[j, rows, :]
                highest = jnp.maximum(highest, before[:, :1])
            weights = jnp.exp2((scores - highest) * SCALE2).astype(jnp.bfloat16)
            both = jnp.dot(weights, vx_ref[...], preferred_element_type=jnp.float32)
            acc, denominator = both[:, :HD], both[:, HD:]
            if not first:
                keep = jnp.exp2((before - highest) * SCALE2)
                acc = acc + keep * acc_in[j, rows, :]
                denominator = denominator + keep * den_in[j, rows, :]
            if last:
                out_ref[j ^ place_ref[5], rows, :] = (acc / denominator).astype(jnp.bfloat16)
                stats.append(highest * SCALE2 + jnp.log2(denominator))
            else:
                acc_out[j, rows, :] = acc
                top_out[j, rows, :] = jnp.broadcast_to(highest, (ROWS, HD))
                den_out[j, rows, :] = denominator
        if last:
            which = lane % GROUP
            level = jnp.where(which == 0, stats[0], jnp.where(which == 1, stats[1], stats[2]))
            high = level.astype(jnp.bfloat16).astype(jnp.float32)
            rest = level - high
            middle = rest.astype(jnp.bfloat16).astype(jnp.float32)
            parts = jnp.where(lane < GROUP, high, jnp.where(lane < 2 * GROUP, middle, rest - middle))
            out_ref[j ^ place_ref[5], pl.ds(QROWS, STAT), :] = parts.T[:STAT].astype(jnp.bfloat16)
        return carry

    for j in range(4):
        one_shard(j, 0)


def attend(place, qa, qb, masks, kvs, state=None, last=False):
    chunks = len(kvs)
    vmem = pl.BlockSpec(memory_space=pltpu.VMEM)
    if last:
        outs = jax.ShapeDtypeStruct((4, QROWS + STAT, HD), jnp.bfloat16)
        out_specs = vmem
    else:
        outs = [jax.ShapeDtypeStruct((4, QROWS, HD), jnp.float32)] * 3
        out_specs = [vmem] * 3
    args = (place, qa, qb, masks, *kvs) + (tuple(state) if state is not None else ())
    keys = chunks * FAR * ROWS
    return pl.pallas_call(
        functools.partial(attend_kernel, state is None, last, chunks),
        out_shape=outs,
        in_specs=[pl.BlockSpec(memory_space=pltpu.SMEM)] + [vmem] * (len(args) - 1),
        out_specs=out_specs,
        scratch_shapes=[
            pltpu.VMEM((4, QROWS, 2 * HD), jnp.bfloat16),
            pltpu.VMEM((2 * HD, keys), jnp.bfloat16),
            pltpu.VMEM((keys, 2 * HD), jnp.bfloat16),
            pltpu.VMEM((4, QROWS, keys), jnp.float32),
        ],
        cost_estimate=pl.CostEstimate(
            flops=4 * 4 * QROWS * keys * HD * 2, bytes_accessed=2**20, transcendentals=4 * QROWS * keys
        ),
        compiler_params=pltpu.CompilerParams(vmem_limit_bytes=32 * 2**20),
        name="attend_last" if last else "attend",
    )(*args)


def combine_kernel(p_ref, out_ref):
    parts = p_ref.shape[0]
    levels = []
    for i in range(parts):
        st = p_ref[i, pl.ds(QROWS, STAT), :].astype(jnp.float32)
        levels.append(st[0:GROUP] + st[GROUP : 2 * GROUP] + st[2 * GROUP : 3 * GROUP])
    top = levels[0]
    for i in range(1, parts):
        top = jnp.maximum(top, levels[i])
    shares = [jnp.exp2(level - top) for level in levels]
    total = shares[0]
    for i in range(1, parts):
        total = total + shares[i]
    shares = [share / total for share in shares]
    pad = jnp.zeros((HD - parts * GROUP, HD), jnp.float32)
    columns = jnp.concatenate(shares + [pad], axis=0).T
    for g in range(GROUP):
        acc = None
        for i in range(parts):
            c = i * GROUP + g
            term = p_ref[i, pl.ds(g * ROWS, ROWS), :].astype(jnp.float32) * columns[:, c : c + 1]
            acc = term if acc is None else acc + term
        out_ref[g] = acc.astype(jnp.bfloat16)


def combine(parts):
    vmem = pl.BlockSpec(memory_space=pltpu.VMEM)
    return pl.pallas_call(
        combine_kernel,
        out_shape=jax.ShapeDtypeStruct((GROUP, ROWS, HD), jnp.bfloat16),
        in_specs=[vmem],
        out_specs=vmem,
        compiler_params=pltpu.CompilerParams(vmem_limit_bytes=16 * 2**20),
        name="combine",
    )(parts)


def swap(value, axis):
    return lax.ppermute(value, axis, [(0, 1), (1, 0)])


def per_device(queries, key_states, value_states, head_masks):
    c, yh, zs, z0, ys, y0 = (lax.axis_index(a) for a in PLANE)
    y, z = yh * 4 + ys * 2 + y0, zs * 2 + z0

    kv = jnp.stack([key_states[0, 0], value_states[0, 0]])
    kv = kv.transpose(2, 0, 1, 3).reshape(4, 2, 2, 16, HD)
    even, odd = kv[:, 0], kv[:, 1]
    give = jnp.where(c == 0, odd, even)
    got = swap(give, "c")
    low = jnp.where(c == 0, even, got)
    high = jnp.where(c == 0, got, odd)
    kv = jnp.stack([low, high], axis=1)
    kv = jnp.broadcast_to(kv[:, None], (4, FAR, 2, 2, 16, HD)).reshape(4 * FAR, 2, 2, 16, HD)
    own = lax.all_to_all(kv, AXES, 0, 0, axis_index_groups=first_axis_groups(), tiled=True)

    mine = queries.transpose(1, 0, 2)
    qa = jnp.stack([mine, swap(mine, "y0")])
    qb = swap(qa, "z0")

    down = lax.ppermute(own, PLANE, second_axis_shift(3))
    up = lax.ppermute(own, PLANE, second_axis_shift(1))
    far = lax.ppermute(down, PLANE, second_axis_shift(3))
    shape = (4, FAR, 2, 2, 16, HD)
    chunk = {r: a.reshape(shape) for r, a in ((0, own), (1, up), (3, down), (2, far))}

    q_shards = [shard_of(y ^ (j & 1), z ^ (j >> 1)) for j in range(4)]
    k_shards = []
    for r in (0, 1, 3, 2):
        for k in range(FAR):
            yk = jnp.where(c == 0, (y - 2 * r) & 7, 2 * k + y0)
            zk = jnp.where(c == 0, 2 * k + z0, (z - 2 * r) & 7)
            k_shards.append(shard_of(yk, zk))
    own_place = jnp.where(c == 0, z >> 1, y >> 1)
    me = z0 * 2 + y0
    zero = jnp.int32(0)
    place = jnp.stack([own_place, *q_shards, me, zero, zero, *k_shards]).astype(jnp.int32)

    state = attend(place, qa, qb, head_masks, [chunk[0], chunk[1], chunk[3]])
    parts = attend(place, qa, qb, head_masks, [chunk[2]], state, last=True)
    parts = lax.all_to_all(parts, BLOCK, 0, 0, tiled=True)
    return combine(parts).transpose(1, 0, 2)


def solution(mesh):
    fine = Mesh(mesh.devices.reshape(SIZES), AXES)
    return jax.shard_map(
        per_device,
        mesh=fine,
        in_specs=(P(TOK, HEAD, None), P(TOK, HEAD), P(TOK, HEAD), P(HEAD)),
        out_specs=P(TOK, HEAD, None),
        check_vma=False,
    )
```

```python
import functools

import jax
import jax.numpy as jnp
from jax import lax
from jax.experimental import pallas as pl
from jax.experimental.pallas import tpu as pltpu
from jax.sharding import Mesh, PartitionSpec as P

HEAD = ("x", "c")
TOK = ("yh", "zs", "z0", "ys", "y0")
BLOCK = ("z0", "y0")
AXES = HEAD + TOK
PLANE = ("c",) + TOK
SIZES = (4, 2, 2, 4, 2, 2, 2)

HD = 128
ROWS = 128
GROUP = 3
QROWS = GROUP * ROWS
STAT = 16
BLK = 64
FAR = 4
MASKED = -1e30
LOG2E = 1.4426950408889634
CHUNKS = 8
SCALE2 = HD**-0.5 * LOG2E


def plane_index(c, y, z):
    return c * 64 + (y >> 2) * 32 + z * 4 + (y & 3)


def plane_places():
    return [(c, y, z) for c in range(2) for y in range(8) for z in range(8)]


def second_axis_xor(bits):
    pairs = []
    for c, y, z in plane_places():
        to = (y ^ bits, z) if c == 0 else (y, z ^ bits)
        pairs.append((plane_index(c, y, z), plane_index(c, *to)))
    return pairs


def first_axis_groups():
    groups = {}
    for x in range(4):
        for c, y, z in plane_places():
            key = (c, y, z & 1) if c == 0 else (c, y & 1, z)
            groups.setdefault(key, []).append(x * 128 + plane_index(c, y, z))
    return list(groups.values())


def shard_of(y, z):
    return (y >> 2) * 32 + z * 4 + (y & 3)


def load_operands(base, place_ref, qa_ref, qb_ref, mask_ref, kv_refs, qx_ref, kx_ref, vx_ref):
    lane = lax.broadcasted_iota(jnp.int32, (ROWS, HD), 1)
    row = lax.broadcasted_iota(jnp.int32, (ROWS, HD), 0)
    row_half = row // BLK
    for n, kv_ref in enumerate(kv_refs):
        for k in range(FAR):
            s = n * FAR + k
            rows = pl.ds(s * ROWS, ROWS)
            kx_ref[:HD, rows] = kv_ref[:, k, :, 0].reshape(ROWS, HD).T
            vx_ref[rows, :HD] = kv_ref[:, k, :, 1].reshape(ROWS, HD)
            block = 2 * place_ref[base + s] + lane // BLK
            kx_ref[HD:, rows] = jnp.where(row == block, 1.0, 0.0).astype(jnp.bfloat16)
            vx_ref[rows, HD:] = jnp.ones((ROWS, HD), jnp.bfloat16)
    for j in range(4):
        src = (qa_ref, qb_ref)[j >> 1]
        shard = place_ref[1 + j]
        qx_ref[j, :, :HD] = src[j & 1].reshape(QROWS, HD)
        for g in range(GROUP):
            for half in range(2):
                bias = jnp.where(mask_ref[g, pl.ds(2 * shard + half, 1), :] > 0, 0.0, MASKED)
                rows = pl.ds(g * ROWS + half * BLK, BLK)
                qx_ref[j, rows, HD:] = jnp.broadcast_to(bias, (BLK, HD)).astype(jnp.bfloat16)
    return lane, row


def attend_kernel(chunks, place_ref, qa_ref, qb_ref, mask_ref, *refs):
    kv_refs, (acc_out, top_out, den_out, qx_ref, kx_ref, vx_ref, s_ref, p_ref) = refs[:chunks], refs[chunks:]
    lane, row = load_operands(CHUNKS, place_ref, qa_ref, qb_ref, mask_ref, kv_refs, qx_ref, kx_ref, vx_ref)
    tops = {}
    for j in range(4):
        s_ref[j] = jnp.dot(qx_ref[j], kx_ref[...], preferred_element_type=jnp.float32)
    cols = pl.ds(pl.multiple_of(place_ref[0] * ROWS, ROWS), ROWS)
    for g in range(GROUP):
        rows = pl.ds(g * ROWS, ROWS)
        s_ref[0, rows, cols] = jnp.where(lane <= row, s_ref[0, rows, cols], MASKED)
    for j in range(4):
        for g in range(GROUP):
            rows = pl.ds(g * ROWS, ROWS)
            tops[j, g] = jnp.max(s_ref[j, rows, :], axis=1, keepdims=True)
    for j in range(4):
        for g in range(GROUP):
            rows = pl.ds(g * ROWS, ROWS)
            p_ref[j, rows, :] = jnp.exp2((s_ref[j, rows, :] - tops[j, g]) * SCALE2).astype(jnp.bfloat16)
    for j in range(4):
        both = jnp.dot(p_ref[j], vx_ref[...], preferred_element_type=jnp.float32)
        acc_out[j] = both[:, :HD]
        den_out[j] = both[:, HD:]
        for g in range(GROUP):
            top_out[j, pl.ds(g * ROWS, ROWS), :] = jnp.broadcast_to(tops[j, g], (ROWS, HD))


def attend_last_kernel(
    place_ref, qa_ref, qb_ref, mask_ref, kv_ref, acc_in, top_in, den_in, out_ref, qx_ref, kx_ref, vx_ref, s_ref
):
    base = CHUNKS + 3 * FAR
    lane, _ = load_operands(base, place_ref, qa_ref, qb_ref, mask_ref, [kv_ref], qx_ref, kx_ref, vx_ref)
    for j in range(4):
        s_ref[j] = jnp.dot(qx_ref[j], kx_ref[...], preferred_element_type=jnp.float32)
        slot = j ^ place_ref[5]
        stats = []
        for g in range(GROUP):
            rows = pl.ds(g * ROWS, ROWS)
            scores = s_ref[j, rows, :]
            before = top_in[j, rows, :]
            highest = jnp.maximum(jnp.max(scores, axis=1, keepdims=True), before[:, :1])
            weights = jnp.exp2((scores - highest) * SCALE2).astype(jnp.bfloat16)
            both = jnp.dot(weights, vx_ref[...], preferred_element_type=jnp.float32)
            keep = jnp.exp2((before - highest) * SCALE2)
            acc = both[:, :HD] + keep * acc_in[j, rows, :]
            denominator = both[:, HD:] + keep * den_in[j, rows, :]
            out_ref[slot, rows, :] = (acc / denominator).astype(jnp.bfloat16)
            stats.append(highest * SCALE2 + jnp.log2(denominator))
        which = lane % GROUP
        level = jnp.where(which == 0, stats[0], jnp.where(which == 1, stats[1], stats[2]))
        high = level.astype(jnp.bfloat16).astype(jnp.float32)
        rest = level - high
        middle = rest.astype(jnp.bfloat16).astype(jnp.float32)
        parts = jnp.where(lane < GROUP, high, jnp.where(lane < 2 * GROUP, middle, rest - middle))
        out_ref[slot, pl.ds(QROWS, STAT), :] = parts.T[:STAT].astype(jnp.bfloat16)


def attend(place, qa, qb, masks, kvs, state=None):
    vmem = pl.BlockSpec(memory_space=pltpu.VMEM)
    keys = len(kvs) * FAR * ROWS
    scratch = [
        pltpu.VMEM((4, QROWS, 2 * HD), jnp.bfloat16),
        pltpu.VMEM((2 * HD, keys), jnp.bfloat16),
        pltpu.VMEM((keys, 2 * HD), jnp.bfloat16),
        pltpu.VMEM((4, QROWS, keys), jnp.float32),
    ]
    if state is None:
        kernel, name, state = functools.partial(attend_kernel, len(kvs)), "attend", ()
        outs = [jax.ShapeDtypeStruct((4, QROWS, HD), jnp.float32)] * 3
        scratch.append(pltpu.VMEM((4, QROWS, keys), jnp.bfloat16))
    else:
        kernel, name = attend_last_kernel, "attend_last"
        outs = jax.ShapeDtypeStruct((4, QROWS + STAT, HD), jnp.bfloat16)
    args = (place, qa, qb, masks, *kvs, *state)
    return pl.pallas_call(
        kernel,
        out_shape=outs,
        in_specs=[pl.BlockSpec(memory_space=pltpu.SMEM)] + [vmem] * (len(args) - 1),
        out_specs=[vmem] * 3 if isinstance(outs, list) else vmem,
        scratch_shapes=scratch,
        cost_estimate=pl.CostEstimate(
            flops=4 * 4 * QROWS * keys * HD * 2, bytes_accessed=2**20, transcendentals=4 * QROWS * keys
        ),
        compiler_params=pltpu.CompilerParams(vmem_limit_bytes=32 * 2**20),
        name=name,
    )(*args)


def combine_kernel(p_ref, out_ref):
    parts = p_ref.shape[0]
    levels = []
    for i in range(parts):
        st = p_ref[i, pl.ds(QROWS, STAT), :].astype(jnp.float32)
        levels.append(st[0:GROUP] + st[GROUP : 2 * GROUP] + st[2 * GROUP : 3 * GROUP])
    top = levels[0]
    for i in range(1, parts):
        top = jnp.maximum(top, levels[i])
    shares = [jnp.exp2(level - top) for level in levels]
    total = shares[0]
    for i in range(1, parts):
        total = total + shares[i]
    shares = [share / total for share in shares]
    pad = jnp.zeros((HD - parts * GROUP, HD), jnp.float32)
    columns = jnp.concatenate(shares + [pad], axis=0).T
    for g in range(GROUP):
        acc = None
        for i in range(parts):
            c = i * GROUP + g
            term = p_ref[i, pl.ds(g * ROWS, ROWS), :].astype(jnp.float32) * columns[:, c : c + 1]
            acc = term if acc is None else acc + term
        out_ref[g] = acc.astype(jnp.bfloat16)


def combine(parts):
    vmem = pl.BlockSpec(memory_space=pltpu.VMEM)
    return pl.pallas_call(
        combine_kernel,
        out_shape=jax.ShapeDtypeStruct((GROUP, ROWS, HD), jnp.bfloat16),
        in_specs=[vmem],
        out_specs=vmem,
        compiler_params=pltpu.CompilerParams(vmem_limit_bytes=16 * 2**20),
        name="combine",
    )(parts)


def swap(value, axis):
    return lax.ppermute(value, axis, [(0, 1), (1, 0)])


def per_device(queries, key_states, value_states, head_masks):
    c, yh, zs, z0, ys, y0 = (lax.axis_index(a) for a in PLANE)
    y, z = yh * 4 + ys * 2 + y0, zs * 2 + z0

    kv = jnp.stack([key_states[0, 0], value_states[0, 0]])
    kv = kv.transpose(2, 0, 1, 3).reshape(4, 2, 2, 16, HD)
    even, odd = kv[:, 0], kv[:, 1]
    give = jnp.where(c == 0, odd, even)
    got = swap(give, "c")
    low = jnp.where(c == 0, even, got)
    high = jnp.where(c == 0, got, odd)
    kv = jnp.stack([low, high], axis=1)
    kv = jnp.broadcast_to(kv[:, None], (4, FAR, 2, 2, 16, HD)).reshape(4 * FAR, 2, 2, 16, HD)
    own = lax.all_to_all(kv, AXES, 0, 0, axis_index_groups=first_axis_groups(), tiled=True)

    mine = queries.transpose(1, 0, 2)
    qa = jnp.stack([mine, swap(mine, "y0")])
    qb = swap(qa, "z0")

    low = lax.ppermute(own, PLANE, second_axis_xor(6))
    high = lax.ppermute(own, PLANE, second_axis_xor(2))
    far = lax.ppermute(low, PLANE, second_axis_xor(2))
    own, low, high, far = (a.reshape(4, FAR, 2, 2, 16, HD) for a in (own, low, high, far))

    q_shards = [shard_of(y ^ (j & 1), z ^ (j >> 1)) for j in range(4)]
    k_shards = []
    for bits in (0, 2, 6, 4):
        for k in range(FAR):
            yk = jnp.where(c == 0, y ^ bits, 2 * k + y0)
            zk = jnp.where(c == 0, 2 * k + z0, z ^ bits)
            k_shards.append(shard_of(yk, zk))
    own_place = jnp.where(c == 0, z >> 1, y >> 1)
    me = z0 * 2 + y0
    zero = jnp.int32(0)
    place = jnp.stack([own_place, *q_shards, me, zero, zero, *k_shards]).astype(jnp.int32)

    state = attend(place, qa, qb, head_masks, [own, high, low])
    parts = attend(place, qa, qb, head_masks, [far], state)
    parts = lax.all_to_all(parts, BLOCK, 0, 0, tiled=True)
    return combine(parts).transpose(1, 0, 2)


def solution(mesh):
    fine = Mesh(mesh.devices.reshape(SIZES), AXES)
    return jax.shard_map(
        per_device,
        mesh=fine,
        in_specs=(P(TOK, HEAD, None), P(TOK, HEAD), P(TOK, HEAD), P(HEAD)),
        out_specs=P(TOK, HEAD, None),
        check_vma=False,
    )
```

```python
import functools

import jax
import jax.numpy as jnp
from jax import lax
from jax.experimental import pallas as pl
from jax.experimental.pallas import tpu as pltpu
from jax.sharding import Mesh, PartitionSpec as P

HEAD = ("x", "c")
TOK = ("yh", "zs", "z0", "ys", "y0")
BLOCK = ("z0", "y0")
AXES = HEAD + TOK
PLANE = ("c",) + TOK
SIZES = (4, 2, 2, 4, 2, 2, 2)

HD = 128
ROWS = 128
GROUP = 3
QROWS = GROUP * ROWS
STAT = 16
BLK = 64
FAR = 4
MASKED = -1e30
LOG2E = 1.4426950408889634
CHUNKS = 8
SCALE2 = HD**-0.5 * LOG2E


def plane_index(c, y, z):
    return c * 64 + (y >> 2) * 32 + z * 4 + (y & 3)


def plane_places():
    return [(c, y, z) for c in range(2) for y in range(8) for z in range(8)]


def second_axis_xor(bits):
    pairs = []
    for c, y, z in plane_places():
        to = (y ^ bits, z) if c == 0 else (y, z ^ bits)
        pairs.append((plane_index(c, y, z), plane_index(c, *to)))
    return pairs


def first_axis_groups():
    groups = {}
    for x in range(4):
        for c, y, z in plane_places():
            key = (c, y, z & 1) if c == 0 else (c, y & 1, z)
            groups.setdefault(key, []).append(x * 128 + plane_index(c, y, z))
    return list(groups.values())


def shard_of(y, z):
    return (y >> 2) * 32 + z * 4 + (y & 3)


def load_operands(base, place_ref, qa_ref, qb_ref, mask_ref, kv_refs, qx_ref, kx_ref, vx_ref):
    lane = lax.broadcasted_iota(jnp.int32, (ROWS, HD), 1)
    row = lax.broadcasted_iota(jnp.int32, (ROWS, HD), 0)
    row_half = row // BLK
    for n, kv_ref in enumerate(kv_refs):
        for k in range(FAR):
            s = n * FAR + k
            rows = pl.ds(s * ROWS, ROWS)
            kx_ref[:HD, rows] = kv_ref[:, k, :, 0].reshape(ROWS, HD).T
            vx_ref[rows, :HD] = kv_ref[:, k, :, 1].reshape(ROWS, HD)
            block = 2 * place_ref[base + s] + lane // BLK
            kx_ref[HD:, rows] = jnp.where(row == block, 1.0, 0.0).astype(jnp.bfloat16)
            vx_ref[rows, HD:] = jnp.ones((ROWS, HD), jnp.bfloat16)
    for j in range(4):
        src = (qa_ref, qb_ref)[j >> 1]
        shard = place_ref[1 + j]
        qx_ref[j, :, :HD] = src[j & 1].reshape(QROWS, HD)
        for g in range(GROUP):
            for half in range(2):
                bias = jnp.where(mask_ref[g, pl.ds(2 * shard + half, 1), :] > 0, 0.0, MASKED)
                rows = pl.ds(g * ROWS + half * BLK, BLK)
                qx_ref[j, rows, HD:] = jnp.broadcast_to(bias, (BLK, HD)).astype(jnp.bfloat16)
    return lane, row


def attend_kernel(chunks, place_ref, qa_ref, qb_ref, mask_ref, *refs):
    kv_refs, (acc_out, top_out, den_out, qx_ref, kx_ref, vx_ref, s_ref, p_ref) = refs[:chunks], refs[chunks:]
    lane, row = load_operands(CHUNKS, place_ref, qa_ref, qb_ref, mask_ref, kv_refs, qx_ref, kx_ref, vx_ref)
    tops = {}
    for j in range(4):
        s_ref[j] = jnp.dot(qx_ref[j], kx_ref[...], preferred_element_type=jnp.float32)
    cols = pl.ds(pl.multiple_of(place_ref[0] * ROWS, ROWS), ROWS)
    for g in range(GROUP):
        rows = pl.ds(g * ROWS, ROWS)
        s_ref[0, rows, cols] = jnp.where(lane <= row, s_ref[0, rows, cols], MASKED)
    for j in range(4):
        for g in range(GROUP):
            rows = pl.ds(g * ROWS, ROWS)
            tops[j, g] = jnp.max(s_ref[j, rows, :], axis=1, keepdims=True)
    for j in range(4):
        for g in range(GROUP):
            rows = pl.ds(g * ROWS, ROWS)
            p_ref[j, rows, :] = jnp.exp2((s_ref[j, rows, :] - tops[j, g]) * SCALE2).astype(jnp.bfloat16)
    for j in range(4):
        both = jnp.dot(p_ref[j], vx_ref[...], preferred_element_type=jnp.float32)
        acc_out[j] = both[:, :HD]
        den_out[j] = both[:, HD:]
        for g in range(GROUP):
            top_out[j, pl.ds(g * ROWS, ROWS), :] = jnp.broadcast_to(tops[j, g], (ROWS, HD))


def attend_last_kernel(
    place_ref, qa_ref, qb_ref, mask_ref, kv_ref, acc_in, top_in, den_in, out_ref, qx_ref, kx_ref, vx_ref, s_ref
):
    base = CHUNKS + 3 * FAR
    lane, _ = load_operands(base, place_ref, qa_ref, qb_ref, mask_ref, [kv_ref], qx_ref, kx_ref, vx_ref)
    for j in range(4):
        s_ref[j] = jnp.dot(qx_ref[j], kx_ref[...], preferred_element_type=jnp.float32)
    for j in range(4):
        slot = j ^ place_ref[5]
        stats, tops, weights = [], [], []
        for g in range(GROUP):
            rows = pl.ds(g * ROWS, ROWS)
            scores = s_ref[j, rows, :]
            before = top_in[j, rows, :]
            highest = jnp.maximum(jnp.max(scores, axis=1, keepdims=True), before)
            shift = jnp.concatenate([highest] * (scores.shape[1] // HD), axis=1)
            weights.append(jnp.exp2((scores - shift) * SCALE2).astype(jnp.bfloat16))
            tops.append(highest)
        total = jnp.dot(jnp.concatenate(weights, axis=0), vx_ref[...], preferred_element_type=jnp.float32)
        for g in range(GROUP):
            rows = pl.ds(g * ROWS, ROWS)
            both, before, highest = total[g * ROWS : (g + 1) * ROWS], top_in[j, rows, :], tops[g]
            keep = jnp.exp2((before - highest) * SCALE2)
            acc = both[:, :HD] + keep * acc_in[j, rows, :]
            denominator = both[:, HD:] + keep * den_in[j, rows, :]
            out_ref[slot, rows, :] = (acc / denominator).astype(jnp.bfloat16)
            stats.append(highest * SCALE2 + jnp.log2(denominator))
        which = lane % GROUP
        level = jnp.where(which == 0, stats[0], jnp.where(which == 1, stats[1], stats[2]))
        high = level.astype(jnp.bfloat16).astype(jnp.float32)
        rest = level - high
        middle = rest.astype(jnp.bfloat16).astype(jnp.float32)
        parts = jnp.where(lane < GROUP, high, jnp.where(lane < 2 * GROUP, middle, rest - middle))
        out_ref[slot, pl.ds(QROWS, STAT), :] = parts.T[:STAT].astype(jnp.bfloat16)


def attend(place, qa, qb, masks, kvs, state=None):
    vmem = pl.BlockSpec(memory_space=pltpu.VMEM)
    keys = len(kvs) * FAR * ROWS
    scratch = [
        pltpu.VMEM((4, QROWS, 2 * HD), jnp.bfloat16),
        pltpu.VMEM((2 * HD, keys), jnp.bfloat16),
        pltpu.VMEM((keys, 2 * HD), jnp.bfloat16),
        pltpu.VMEM((4, QROWS, keys), jnp.float32),
    ]
    if state is None:
        kernel, name, state = functools.partial(attend_kernel, len(kvs)), "attend", ()
        outs = [jax.ShapeDtypeStruct((4, QROWS, HD), jnp.float32)] * 3
        scratch.append(pltpu.VMEM((4, QROWS, keys), jnp.bfloat16))
    else:
        kernel, name = attend_last_kernel, "attend_last"
        outs = jax.ShapeDtypeStruct((4, QROWS + STAT, HD), jnp.bfloat16)
    args = (place, qa, qb, masks, *kvs, *state)
    return pl.pallas_call(
        kernel,
        out_shape=outs,
        in_specs=[pl.BlockSpec(memory_space=pltpu.SMEM)] + [vmem] * (len(args) - 1),
        out_specs=[vmem] * 3 if isinstance(outs, list) else vmem,
        scratch_shapes=scratch,
        cost_estimate=pl.CostEstimate(
            flops=4 * 4 * QROWS * keys * HD * 2, bytes_accessed=2**20, transcendentals=4 * QROWS * keys
        ),
        compiler_params=pltpu.CompilerParams(vmem_limit_bytes=32 * 2**20),
        name=name,
    )(*args)


def combine_kernel(p_ref, out_ref):
    parts = p_ref.shape[0]
    levels = []
    for i in range(parts):
        st = p_ref[i, pl.ds(QROWS, STAT), :].astype(jnp.float32)
        levels.append(st[0:GROUP] + st[GROUP : 2 * GROUP] + st[2 * GROUP : 3 * GROUP])
    top = levels[0]
    for i in range(1, parts):
        top = jnp.maximum(top, levels[i])
    shares = [jnp.exp2(level - top) for level in levels]
    total = shares[0]
    for i in range(1, parts):
        total = total + shares[i]
    shares = [share / total for share in shares]
    pad = jnp.zeros((HD - parts * GROUP, HD), jnp.float32)
    columns = jnp.concatenate(shares + [pad], axis=0).T
    for g in range(GROUP):
        acc = None
        for i in range(parts):
            c = i * GROUP + g
            term = p_ref[i, pl.ds(g * ROWS, ROWS), :].astype(jnp.float32) * columns[:, c : c + 1]
            acc = term if acc is None else acc + term
        out_ref[g] = acc.astype(jnp.bfloat16)


def combine(parts):
    vmem = pl.BlockSpec(memory_space=pltpu.VMEM)
    return pl.pallas_call(
        combine_kernel,
        out_shape=jax.ShapeDtypeStruct((GROUP, ROWS, HD), jnp.bfloat16),
        in_specs=[vmem],
        out_specs=vmem,
        compiler_params=pltpu.CompilerParams(vmem_limit_bytes=16 * 2**20),
        name="combine",
    )(parts)


def swap(value, axis):
    return lax.ppermute(value, axis, [(0, 1), (1, 0)])


def per_device(queries, key_states, value_states, head_masks):
    c, yh, zs, z0, ys, y0 = (lax.axis_index(a) for a in PLANE)
    y, z = yh * 4 + ys * 2 + y0, zs * 2 + z0

    kv = jnp.stack([key_states[0, 0], value_states[0, 0]])
    kv = kv.transpose(2, 0, 1, 3).reshape(4, 2, 2, 16, HD)
    even, odd = kv[:, 0], kv[:, 1]
    give = jnp.where(c == 0, odd, even)
    got = swap(give, "c")
    low = jnp.where(c == 0, even, got)
    high = jnp.where(c == 0, got, odd)
    kv = jnp.stack([low, high], axis=1)
    kv = jnp.broadcast_to(kv[:, None], (4, FAR, 2, 2, 16, HD)).reshape(4 * FAR, 2, 2, 16, HD)
    own = lax.all_to_all(kv, AXES, 0, 0, axis_index_groups=first_axis_groups(), tiled=True)

    mine = queries.transpose(1, 0, 2)
    qa = jnp.stack([mine, swap(mine, "y0")])
    qb = swap(qa, "z0")

    low = lax.ppermute(own, PLANE, second_axis_xor(6))
    high = lax.ppermute(own, PLANE, second_axis_xor(2))
    far = lax.ppermute(low, PLANE, second_axis_xor(2))
    own, low, high, far = (a.reshape(4, FAR, 2, 2, 16, HD) for a in (own, low, high, far))

    q_shards = [shard_of(y ^ (j & 1), z ^ (j >> 1)) for j in range(4)]
    k_shards = []
    for bits in (0, 2, 6, 4):
        for k in range(FAR):
            yk = jnp.where(c == 0, y ^ bits, 2 * k + y0)
            zk = jnp.where(c == 0, 2 * k + z0, z ^ bits)
            k_shards.append(shard_of(yk, zk))
    own_place = jnp.where(c == 0, z >> 1, y >> 1)
    me = z0 * 2 + y0
    zero = jnp.int32(0)
    place = jnp.stack([own_place, *q_shards, me, zero, zero, *k_shards]).astype(jnp.int32)

    state = attend(place, qa, qb, head_masks, [own, high, low])
    parts = attend(place, qa, qb, head_masks, [far], state)
    parts = lax.all_to_all(parts, BLOCK, 0, 0, tiled=True)
    return combine(parts).transpose(1, 0, 2)


def solution(mesh):
    fine = Mesh(mesh.devices.reshape(SIZES), AXES)
    return jax.shard_map(
        per_device,
        mesh=fine,
        in_specs=(P(TOK, HEAD, None), P(TOK, HEAD), P(TOK, HEAD), P(HEAD)),
        out_specs=P(TOK, HEAD, None),
        check_vma=False,
    )
```

```python
import functools

import jax
import jax.numpy as jnp
from jax import lax
from jax.experimental import pallas as pl
from jax.experimental.pallas import tpu as pltpu
from jax.sharding import Mesh, PartitionSpec as P

HEAD = ("x", "c")
TOK = ("yh", "zs", "z0", "ys", "y0")
BLOCK = ("z0", "y0")
AXES = HEAD + TOK
PLANE = ("c",) + TOK
SIZES = (4, 2, 2, 4, 2, 2, 2)

HD = 128
ROWS = 128
GROUP = 3
QROWS = GROUP * ROWS
STAT = 16
BLK = 64
FAR = 4
MASKED = -1e30
LOG2E = 1.4426950408889634
CHUNKS = 8
SCALE2 = HD**-0.5 * LOG2E


def plane_index(c, y, z):
    return c * 64 + (y >> 2) * 32 + z * 4 + (y & 3)


def plane_places():
    return [(c, y, z) for c in range(2) for y in range(8) for z in range(8)]


def second_axis_xor(bits, relay=False):
    pairs = []
    for c, y, z in plane_places():
        to = (y ^ bits, z) if c == 0 else (y, z ^ bits)
        if c == 1 or (y >= 4 if relay else to[0] >= 4 or y < 4):
            pairs.append((plane_index(c, y, z), plane_index(c, *to)))
    return pairs


def first_axis_groups():
    groups = {}
    for x in range(4):
        for c, y, z in plane_places():
            key = (c, y, z & 1) if c == 0 else (c, y & 1, z)
            groups.setdefault(key, []).append(x * 128 + plane_index(c, y, z))
    return list(groups.values())


def shard_of(y, z):
    return (y >> 2) * 32 + z * 4 + (y & 3)


def load_operands(base, place_ref, qa_ref, qb_ref, mask_ref, kv_refs, qx_ref, kx_ref, vx_ref):
    lane = lax.broadcasted_iota(jnp.int32, (ROWS, HD), 1)
    row = lax.broadcasted_iota(jnp.int32, (ROWS, HD), 0)
    row_half = row // BLK
    for n, kv_ref in enumerate(kv_refs):
        for k in range(FAR):
            s = n * FAR + k
            rows = pl.ds(s * ROWS, ROWS)
            kx_ref[:HD, rows] = kv_ref[:, k, :, 0].reshape(ROWS, HD).T
            vx_ref[rows, :HD] = kv_ref[:, k, :, 1].reshape(ROWS, HD)
            block = 2 * place_ref[base + s] + lane // BLK
            kx_ref[HD:, rows] = jnp.where(row == block, 1.0, 0.0).astype(jnp.bfloat16)
            vx_ref[rows, HD:] = jnp.ones((ROWS, HD), jnp.bfloat16)
    for j in range(4):
        src = (qa_ref, qb_ref)[j >> 1]
        shard = place_ref[1 + j]
        qx_ref[j, :, :HD] = src[j & 1].reshape(QROWS, HD)
        for g in range(GROUP):
            for half in range(2):
                bias = jnp.where(mask_ref[g, pl.ds(2 * shard + half, 1), :] > 0, 0.0, MASKED)
                rows = pl.ds(g * ROWS + half * BLK, BLK)
                qx_ref[j, rows, HD:] = jnp.broadcast_to(bias, (BLK, HD)).astype(jnp.bfloat16)
    return lane, row


def attend_kernel(chunks, place_ref, qa_ref, qb_ref, mask_ref, *refs):
    kv_refs, (acc_out, top_out, den_out, qx_ref, kx_ref, vx_ref, s_ref, p_ref) = refs[:chunks], refs[chunks:]
    lane, row = load_operands(CHUNKS, place_ref, qa_ref, qb_ref, mask_ref, kv_refs, qx_ref, kx_ref, vx_ref)
    tops = {}
    for j in range(4):
        s_ref[j] = jnp.dot(qx_ref[j], kx_ref[...], preferred_element_type=jnp.float32)
    cols = pl.ds(pl.multiple_of(place_ref[0] * ROWS, ROWS), ROWS)
    for g in range(GROUP):
        rows = pl.ds(g * ROWS, ROWS)
        s_ref[0, rows, cols] = jnp.where(lane <= row, s_ref[0, rows, cols], MASKED)
    for j in range(4):
        for g in range(GROUP):
            rows = pl.ds(g * ROWS, ROWS)
            tops[j, g] = jnp.max(s_ref[j, rows, :], axis=1, keepdims=True)
    for j in range(4):
        for g in range(GROUP):
            rows = pl.ds(g * ROWS, ROWS)
            p_ref[j, rows, :] = jnp.exp2((s_ref[j, rows, :] - tops[j, g]) * SCALE2).astype(jnp.bfloat16)
    for j in range(4):
        both = jnp.dot(p_ref[j], vx_ref[...], preferred_element_type=jnp.float32)
        acc_out[j] = both[:, :HD]
        den_out[j] = both[:, HD:]
        for g in range(GROUP):
            top_out[j, pl.ds(g * ROWS, ROWS), :] = jnp.broadcast_to(tops[j, g], (ROWS, HD))


def attend_last_kernel(
    place_ref, qa_ref, qb_ref, mask_ref, kv_ref, acc_in, top_in, den_in, out_ref, qx_ref, kx_ref, vx_ref, s_ref
):
    base = CHUNKS + 3 * FAR
    lane, _ = load_operands(base, place_ref, qa_ref, qb_ref, mask_ref, [kv_ref], qx_ref, kx_ref, vx_ref)
    for j in range(4):
        s_ref[j] = jnp.dot(qx_ref[j], kx_ref[...], preferred_element_type=jnp.float32)
    for j in range(4):
        slot = j ^ place_ref[5]
        stats, tops, weights = [], [], []
        for g in range(GROUP):
            rows = pl.ds(g * ROWS, ROWS)
            scores = s_ref[j, rows, :]
            before = top_in[j, rows, :]
            highest = jnp.maximum(jnp.max(scores, axis=1, keepdims=True), before)
            shift = jnp.concatenate([highest] * (scores.shape[1] // HD), axis=1)
            weights.append(jnp.exp2((scores - shift) * SCALE2).astype(jnp.bfloat16))
            tops.append(highest)
        total = jnp.dot(jnp.concatenate(weights, axis=0), vx_ref[...], preferred_element_type=jnp.float32)
        for g in range(GROUP):
            rows = pl.ds(g * ROWS, ROWS)
            both, before, highest = total[g * ROWS : (g + 1) * ROWS], top_in[j, rows, :], tops[g]
            keep = jnp.exp2((before - highest) * SCALE2)
            acc = both[:, :HD] + keep * acc_in[j, rows, :]
            denominator = both[:, HD:] + keep * den_in[j, rows, :]
            out_ref[slot, rows, :] = (acc / denominator).astype(jnp.bfloat16)
            stats.append(highest * SCALE2 + jnp.log2(denominator))
        which = lane % GROUP
        level = jnp.where(which == 0, stats[0], jnp.where(which == 1, stats[1], stats[2]))
        high = level.astype(jnp.bfloat16).astype(jnp.float32)
        rest = level - high
        middle = rest.astype(jnp.bfloat16).astype(jnp.float32)
        parts = jnp.where(lane < GROUP, high, jnp.where(lane < 2 * GROUP, middle, rest - middle))
        out_ref[slot, pl.ds(QROWS, STAT), :] = parts.T[:STAT].astype(jnp.bfloat16)


def attend(place, qa, qb, masks, kvs, state=None):
    vmem = pl.BlockSpec(memory_space=pltpu.VMEM)
    keys = len(kvs) * FAR * ROWS
    scratch = [
        pltpu.VMEM((4, QROWS, 2 * HD), jnp.bfloat16),
        pltpu.VMEM((2 * HD, keys), jnp.bfloat16),
        pltpu.VMEM((keys, 2 * HD), jnp.bfloat16),
        pltpu.VMEM((4, QROWS, keys), jnp.float32),
    ]
    if state is None:
        kernel, name, state = functools.partial(attend_kernel, len(kvs)), "attend", ()
        outs = [jax.ShapeDtypeStruct((4, QROWS, HD), jnp.float32)] * 3
        scratch.append(pltpu.VMEM((4, QROWS, keys), jnp.bfloat16))
    else:
        kernel, name = attend_last_kernel, "attend_last"
        outs = jax.ShapeDtypeStruct((4, QROWS + STAT, HD), jnp.bfloat16)
    args = (place, qa, qb, masks, *kvs, *state)
    return pl.pallas_call(
        kernel,
        out_shape=outs,
        in_specs=[pl.BlockSpec(memory_space=pltpu.SMEM)] + [vmem] * (len(args) - 1),
        out_specs=[vmem] * 3 if isinstance(outs, list) else vmem,
        scratch_shapes=scratch,
        cost_estimate=pl.CostEstimate(
            flops=4 * 4 * QROWS * keys * HD * 2, bytes_accessed=2**20, transcendentals=4 * QROWS * keys
        ),
        compiler_params=pltpu.CompilerParams(vmem_limit_bytes=32 * 2**20),
        name=name,
    )(*args)


def combine_kernel(p_ref, out_ref):
    parts = p_ref.shape[0]
    levels = []
    for i in range(parts):
        st = p_ref[i, pl.ds(QROWS, STAT), :].astype(jnp.float32)
        levels.append(st[0:GROUP] + st[GROUP : 2 * GROUP] + st[2 * GROUP : 3 * GROUP])
    top = levels[0]
    for i in range(1, parts):
        top = jnp.maximum(top, levels[i])
    shares = [jnp.exp2(level - top) for level in levels]
    total = shares[0]
    for i in range(1, parts):
        total = total + shares[i]
    shares = [share / total for share in shares]
    pad = jnp.zeros((HD - parts * GROUP, HD), jnp.float32)
    columns = jnp.concatenate(shares + [pad], axis=0).T
    for g in range(GROUP):
        acc = None
        for i in range(parts):
            c = i * GROUP + g
            term = p_ref[i, pl.ds(g * ROWS, ROWS), :].astype(jnp.float32) * columns[:, c : c + 1]
            acc = term if acc is None else acc + term
        out_ref[g] = acc.astype(jnp.bfloat16)


def combine(parts):
    vmem = pl.BlockSpec(memory_space=pltpu.VMEM)
    return pl.pallas_call(
        combine_kernel,
        out_shape=jax.ShapeDtypeStruct((GROUP, ROWS, HD), jnp.bfloat16),
        in_specs=[vmem],
        out_specs=vmem,
        compiler_params=pltpu.CompilerParams(vmem_limit_bytes=16 * 2**20),
        name="combine",
    )(parts)


def swap(value, axis):
    return lax.ppermute(value, axis, [(0, 1), (1, 0)])


def per_device(queries, key_states, value_states, head_masks):
    c, yh, zs, z0, ys, y0 = (lax.axis_index(a) for a in PLANE)
    y, z = yh * 4 + ys * 2 + y0, zs * 2 + z0

    kv = jnp.stack([key_states[0, 0], value_states[0, 0]])
    kv = kv.transpose(2, 0, 1, 3).reshape(4, 2, 2, 16, HD)
    even, odd = kv[:, 0], kv[:, 1]
    give = jnp.where(c == 0, odd, even)
    got = swap(give, "c")
    low = jnp.where(c == 0, even, got)
    high = jnp.where(c == 0, got, odd)
    kv = jnp.stack([low, high], axis=1)
    kv = jnp.broadcast_to(kv[:, None], (4, FAR, 2, 2, 16, HD)).reshape(4 * FAR, 2, 2, 16, HD)
    own = lax.all_to_all(kv, AXES, 0, 0, axis_index_groups=first_axis_groups(), tiled=True)

    mine = queries.transpose(1, 0, 2)
    qa = jnp.stack([mine, swap(mine, "y0")])
    qb = swap(qa, "z0")

    low = lax.ppermute(own, PLANE, second_axis_xor(6))
    high = lax.ppermute(own, PLANE, second_axis_xor(2))
    far = lax.ppermute(low, PLANE, second_axis_xor(2, relay=True))
    own, low, high, far = (a.reshape(4, FAR, 2, 2, 16, HD) for a in (own, low, high, far))

    q_shards = [shard_of(y ^ (j & 1), z ^ (j >> 1)) for j in range(4)]
    k_shards = []
    for bits in (0, 2, 6, 4):
        for k in range(FAR):
            yk = jnp.where(c == 0, y ^ bits, 2 * k + y0)
            zk = jnp.where(c == 0, 2 * k + z0, z ^ bits)
            k_shards.append(shard_of(yk, zk))
    own_place = jnp.where(c == 0, z >> 1, y >> 1)
    me = z0 * 2 + y0
    zero = jnp.int32(0)
    place = jnp.stack([own_place, *q_shards, me, zero, zero, *k_shards]).astype(jnp.int32)

    state = attend(place, qa, qb, head_masks, [own, high, low])
    parts = attend(place, qa, qb, head_masks, [far], state)
    parts = lax.all_to_all(parts, BLOCK, 0, 0, tiled=True)
    return combine(parts).transpose(1, 0, 2)


def solution(mesh):
    fine = Mesh(mesh.devices.reshape(SIZES), AXES)
    return jax.shard_map(
        per_device,
        mesh=fine,
        in_specs=(P(TOK, HEAD, None), P(TOK, HEAD), P(TOK, HEAD), P(HEAD)),
        out_specs=P(TOK, HEAD, None),
        check_vma=False,
    )
```

```python
import functools

import jax
import jax.numpy as jnp
from jax import lax
from jax.experimental import pallas as pl
from jax.experimental.pallas import tpu as pltpu
from jax.sharding import Mesh, PartitionSpec as P

HEAD = ("x", "c")
TOK = ("yh", "zs", "z0", "ys", "y0")
BLOCK = ("z0", "y0")
AXES = HEAD + TOK
PLANE = ("c",) + TOK
SIZES = (4, 2, 2, 4, 2, 2, 2)

HD = 128
ROWS = 128
GROUP = 3
QROWS = GROUP * ROWS
STAT = 16
BLK = 64
FAR = 4
MASKED = -1e30
LOG2E = 1.4426950408889634
CHUNKS = 8
SCALE2 = HD**-0.5 * LOG2E


def plane_index(c, y, z):
    return c * 64 + (y >> 2) * 32 + z * 4 + (y & 3)


def plane_places():
    return [(c, y, z) for c in range(2) for y in range(8) for z in range(8)]


def second_axis_xor(bits):
    pairs = []
    for c, y, z in plane_places():
        to = (y ^ bits, z) if c == 0 else (y, z ^ bits)
        if c == 1 or to[0] >= 4 or y < 4:
            pairs.append((plane_index(c, y, z), plane_index(c, *to)))
    return pairs


def first_axis_groups():
    groups = {}
    for x in range(4):
        for c, y, z in plane_places():
            key = (c, y, z & 1) if c == 0 else (c, y & 1, z)
            groups.setdefault(key, []).append(x * 128 + plane_index(c, y, z))
    return list(groups.values())


def shard_of(y, z):
    return (y >> 2) * 32 + z * 4 + (y & 3)


def load_operands(base, place_ref, qa_ref, qb_ref, mask_ref, kv_refs, qx_ref, kx_ref, vx_ref):
    lane = lax.broadcasted_iota(jnp.int32, (ROWS, HD), 1)
    row = lax.broadcasted_iota(jnp.int32, (ROWS, HD), 0)
    row_half = row // BLK
    for n, kv_ref in enumerate(kv_refs):
        for k in range(FAR):
            s = n * FAR + k
            rows = pl.ds(s * ROWS, ROWS)
            kx_ref[:HD, rows] = kv_ref[:, k, :, 0].reshape(ROWS, HD).T
            vx_ref[rows, :HD] = kv_ref[:, k, :, 1].reshape(ROWS, HD)
            block = 2 * place_ref[base + s] + lane // BLK
            kx_ref[HD:, rows] = jnp.where(row == block, 1.0, 0.0).astype(jnp.bfloat16)
            vx_ref[rows, HD:] = jnp.ones((ROWS, HD), jnp.bfloat16)
    for j in range(4):
        src = (qa_ref, qb_ref)[j >> 1]
        shard = place_ref[1 + j]
        qx_ref[j, :, :HD] = src[j & 1].reshape(QROWS, HD)
        for g in range(GROUP):
            for half in range(2):
                bias = jnp.where(mask_ref[g, pl.ds(2 * shard + half, 1), :] > 0, 0.0, MASKED)
                rows = pl.ds(g * ROWS + half * BLK, BLK)
                qx_ref[j, rows, HD:] = jnp.broadcast_to(bias, (BLK, HD)).astype(jnp.bfloat16)
    return lane, row


def attend_kernel(chunks, place_ref, qa_ref, qb_ref, mask_ref, *refs):
    kv_refs, (acc_out, top_out, den_out, qx_ref, kx_ref, vx_ref, s_ref, p_ref) = refs[:chunks], refs[chunks:]
    lane, row = load_operands(CHUNKS, place_ref, qa_ref, qb_ref, mask_ref, kv_refs, qx_ref, kx_ref, vx_ref)
    tops = {}
    for j in range(4):
        s_ref[j] = jnp.dot(qx_ref[j], kx_ref[...], preferred_element_type=jnp.float32)
    cols = pl.ds(pl.multiple_of(place_ref[0] * ROWS, ROWS), ROWS)
    for g in range(GROUP):
        rows = pl.ds(g * ROWS, ROWS)
        s_ref[0, rows, cols] = jnp.where(lane <= row, s_ref[0, rows, cols], MASKED)
    for j in range(4):
        for g in range(GROUP):
            rows = pl.ds(g * ROWS, ROWS)
            tops[j, g] = jnp.max(s_ref[j, rows, :], axis=1, keepdims=True)
    for j in range(4):
        for g in range(GROUP):
            rows = pl.ds(g * ROWS, ROWS)
            p_ref[j, rows, :] = jnp.exp2((s_ref[j, rows, :] - tops[j, g]) * SCALE2).astype(jnp.bfloat16)
    for j in range(4):
        both = jnp.dot(p_ref[j], vx_ref[...], preferred_element_type=jnp.float32)
        acc_out[j] = both[:, :HD]
        den_out[j] = both[:, HD:]
        for g in range(GROUP):
            top_out[j, pl.ds(g * ROWS, ROWS), :] = jnp.broadcast_to(tops[j, g], (ROWS, HD))


def attend_last_kernel(
    place_ref, qa_ref, qb_ref, mask_ref, kv_ref, acc_in, top_in, den_in, out_ref, qx_ref, kx_ref, vx_ref, s_ref
):
    base = CHUNKS + 3 * FAR
    lane, _ = load_operands(base, place_ref, qa_ref, qb_ref, mask_ref, [kv_ref], qx_ref, kx_ref, vx_ref)
    for j in range(4):
        s_ref[j] = jnp.dot(qx_ref[j], kx_ref[...], preferred_element_type=jnp.float32)
    for j in range(4):
        slot = j ^ place_ref[5]
        stats, tops, weights = [], [], []
        for g in range(GROUP):
            rows = pl.ds(g * ROWS, ROWS)
            scores = s_ref[j, rows, :]
            before = top_in[j, rows, :]
            highest = jnp.maximum(jnp.max(scores, axis=1, keepdims=True), before)
            shift = jnp.concatenate([highest] * (scores.shape[1] // HD), axis=1)
            weights.append(jnp.exp2((scores - shift) * SCALE2).astype(jnp.bfloat16))
            tops.append(highest)
        total = jnp.dot(jnp.concatenate(weights, axis=0), vx_ref[...], preferred_element_type=jnp.float32)
        for g in range(GROUP):
            rows = pl.ds(g * ROWS, ROWS)
            both, before, highest = total[g * ROWS : (g + 1) * ROWS], top_in[j, rows, :], tops[g]
            keep = jnp.exp2((before - highest) * SCALE2)
            acc = both[:, :HD] + keep * acc_in[j, rows, :]
            denominator = both[:, HD:] + keep * den_in[j, rows, :]
            out_ref[slot, rows, :] = (acc / denominator).astype(jnp.bfloat16)
            stats.append(highest * SCALE2 + jnp.log2(denominator))
        which = lane % GROUP
        level = jnp.where(which == 0, stats[0], jnp.where(which == 1, stats[1], stats[2]))
        high = level.astype(jnp.bfloat16).astype(jnp.float32)
        rest = level - high
        middle = rest.astype(jnp.bfloat16).astype(jnp.float32)
        parts = jnp.where(lane < GROUP, high, jnp.where(lane < 2 * GROUP, middle, rest - middle))
        out_ref[slot, pl.ds(QROWS, STAT), :] = parts.T[:STAT].astype(jnp.bfloat16)


def attend(place, qa, qb, masks, kvs, state=None):
    vmem = pl.BlockSpec(memory_space=pltpu.VMEM)
    keys = len(kvs) * FAR * ROWS
    scratch = [
        pltpu.VMEM((4, QROWS, 2 * HD), jnp.bfloat16),
        pltpu.VMEM((2 * HD, keys), jnp.bfloat16),
        pltpu.VMEM((keys, 2 * HD), jnp.bfloat16),
        pltpu.VMEM((4, QROWS, keys), jnp.float32),
    ]
    if state is None:
        kernel, name, state = functools.partial(attend_kernel, len(kvs)), "attend", ()
        outs = [jax.ShapeDtypeStruct((4, QROWS, HD), jnp.float32)] * 3
        scratch.append(pltpu.VMEM((4, QROWS, keys), jnp.bfloat16))
    else:
        kernel, name = attend_last_kernel, "attend_last"
        outs = jax.ShapeDtypeStruct((4, QROWS + STAT, HD), jnp.bfloat16)
    args = (place, qa, qb, masks, *kvs, *state)
    return pl.pallas_call(
        kernel,
        out_shape=outs,
        in_specs=[pl.BlockSpec(memory_space=pltpu.SMEM)] + [vmem] * (len(args) - 1),
        out_specs=[vmem] * 3 if isinstance(outs, list) else vmem,
        scratch_shapes=scratch,
        cost_estimate=pl.CostEstimate(
            flops=4 * 4 * QROWS * keys * HD * 2, bytes_accessed=2**20, transcendentals=4 * QROWS * keys
        ),
        compiler_params=pltpu.CompilerParams(vmem_limit_bytes=32 * 2**20),
        name=name,
    )(*args)


def combine_kernel(p_ref, out_ref):
    parts = p_ref.shape[0]
    levels = []
    for i in range(parts):
        st = p_ref[i, pl.ds(QROWS, STAT), :].astype(jnp.float32)
        levels.append(st[0:GROUP] + st[GROUP : 2 * GROUP] + st[2 * GROUP : 3 * GROUP])
    top = levels[0]
    for i in range(1, parts):
        top = jnp.maximum(top, levels[i])
    shares = [jnp.exp2(level - top) for level in levels]
    total = shares[0]
    for i in range(1, parts):
        total = total + shares[i]
    shares = [share / total for share in shares]
    pad = jnp.zeros((HD - parts * GROUP, HD), jnp.float32)
    columns = jnp.concatenate(shares + [pad], axis=0).T
    for g in range(GROUP):
        acc = None
        for i in range(parts):
            c = i * GROUP + g
            term = p_ref[i, pl.ds(g * ROWS, ROWS), :].astype(jnp.float32) * columns[:, c : c + 1]
            acc = term if acc is None else acc + term
        out_ref[g] = acc.astype(jnp.bfloat16)


def combine(parts):
    vmem = pl.BlockSpec(memory_space=pltpu.VMEM)
    return pl.pallas_call(
        combine_kernel,
        out_shape=jax.ShapeDtypeStruct((GROUP, ROWS, HD), jnp.bfloat16),
        in_specs=[vmem],
        out_specs=vmem,
        compiler_params=pltpu.CompilerParams(vmem_limit_bytes=16 * 2**20),
        name="combine",
    )(parts)


def swap(value, axis):
    return lax.ppermute(value, axis, [(0, 1), (1, 0)])


def per_device(queries, key_states, value_states, head_masks):
    c, yh, zs, z0, ys, y0 = (lax.axis_index(a) for a in PLANE)
    y, z = yh * 4 + ys * 2 + y0, zs * 2 + z0

    kv = jnp.stack([key_states[0, 0], value_states[0, 0]])
    kv = kv.transpose(2, 0, 1, 3).reshape(4, 2, 2, 16, HD)
    even, odd = kv[:, 0], kv[:, 1]
    give = jnp.where(c == 0, odd, even)
    got = swap(give, "c")
    low = jnp.where(c == 0, even, got)
    high = jnp.where(c == 0, got, odd)
    kv = jnp.stack([low, high], axis=1)
    kv = jnp.broadcast_to(kv[:, None], (4, FAR, 2, 2, 16, HD)).reshape(4 * FAR, 2, 2, 16, HD)
    own = lax.all_to_all(kv, AXES, 0, 0, axis_index_groups=first_axis_groups(), tiled=True)

    mine = queries.transpose(1, 0, 2)
    qa = jnp.stack([mine, swap(mine, "y0")])
    qb = swap(qa, "z0")

    low = lax.ppermute(own, PLANE, second_axis_xor(2))
    high = lax.ppermute(own, PLANE, second_axis_xor(6))
    far = lax.ppermute(low, PLANE, second_axis_xor(6))
    own, low, high, far = (a.reshape(4, FAR, 2, 2, 16, HD) for a in (own, low, high, far))

    q_shards = [shard_of(y ^ (j & 1), z ^ (j >> 1)) for j in range(4)]
    k_shards = []
    for bits in (0, 6, 2, 4):
        for k in range(FAR):
            yk = jnp.where(c == 0, y ^ bits, 2 * k + y0)
            zk = jnp.where(c == 0, 2 * k + z0, z ^ bits)
            k_shards.append(shard_of(yk, zk))
    own_place = jnp.where(c == 0, z >> 1, y >> 1)
    me = z0 * 2 + y0
    zero = jnp.int32(0)
    place = jnp.stack([own_place, *q_shards, me, zero, zero, *k_shards]).astype(jnp.int32)

    state = attend(place, qa, qb, head_masks, [own, high, low])
    parts = attend(place, qa, qb, head_masks, [far], state)
    parts = lax.all_to_all(parts, BLOCK, 0, 0, tiled=True)
    return combine(parts).transpose(1, 0, 2)


def solution(mesh):
    fine = Mesh(mesh.devices.reshape(SIZES), AXES)
    return jax.shard_map(
        per_device,
        mesh=fine,
        in_specs=(P(TOK, HEAD, None), P(TOK, HEAD), P(TOK, HEAD), P(HEAD)),
        out_specs=P(TOK, HEAD, None),
        check_vma=False,
    )
```

```python
import functools

import jax
import jax.numpy as jnp
from jax import lax
from jax.experimental import pallas as pl
from jax.experimental.pallas import tpu as pltpu
from jax.sharding import Mesh, PartitionSpec as P

HEAD = ("x", "c")
TOK = ("yh", "zs", "z0", "ys", "y0")
BLOCK = ("z0", "y0")
AXES = HEAD + TOK
PLANE = ("c",) + TOK
SIZES = (4, 2, 2, 4, 2, 2, 2)

HD = 128
ROWS = 128
GROUP = 3
QROWS = GROUP * ROWS
STAT = 16
BLK = 64
FAR = 4
MASKED = -1e30
LOG2E = 1.4426950408889634
CHUNKS = 8
SCALE2 = HD**-0.5 * LOG2E


def plane_index(c, y, z):
    return c * 64 + (y >> 2) * 32 + z * 4 + (y & 3)


def plane_places():
    return [(c, y, z) for c in range(2) for y in range(8) for z in range(8)]


def second_axis_xor(bits, relay=False):
    pairs = []
    for c, y, z in plane_places():
        to = (y ^ bits, z) if c == 0 else (y, z ^ bits)
        if c == 1 or (y >= 4 if relay else to[0] >= 4 or y < 4):
            pairs.append((plane_index(c, y, z), plane_index(c, *to)))
    return pairs


def first_axis_groups():
    groups = {}
    for x in range(4):
        for c, y, z in plane_places():
            key = (c, y, z & 1) if c == 0 else (c, y & 1, z)
            groups.setdefault(key, []).append(x * 128 + plane_index(c, y, z))
    return list(groups.values())


def shard_of(y, z):
    return (y >> 2) * 32 + z * 4 + (y & 3)


def load_operands(base, place_ref, qa_ref, qb_ref, mask_ref, kv_refs, qx_ref, kx_ref, vx_ref):
    lane = lax.broadcasted_iota(jnp.int32, (ROWS, HD), 1)
    row = lax.broadcasted_iota(jnp.int32, (ROWS, HD), 0)
    row_half = row // BLK
    for n, kv_ref in enumerate(kv_refs):
        for k in range(FAR):
            s = n * FAR + k
            rows = pl.ds(s * ROWS, ROWS)
            kx_ref[:HD, rows] = kv_ref[:, k, :, 0].reshape(ROWS, HD).T
            vx_ref[rows, :HD] = kv_ref[:, k, :, 1].reshape(ROWS, HD)
            block = 2 * place_ref[base + s] + lane // BLK
            kx_ref[HD:, rows] = jnp.where(row == block, 1.0, 0.0).astype(jnp.bfloat16)
            vx_ref[rows, HD:] = jnp.ones((ROWS, HD), jnp.bfloat16)
    for j in range(4):
        src = (qa_ref, qb_ref)[j >> 1]
        shard = place_ref[1 + j]
        qx_ref[j, :, :HD] = src[j & 1].reshape(QROWS, HD)
        for g in range(GROUP):
            for half in range(2):
                bias = jnp.where(mask_ref[g, pl.ds(2 * shard + half, 1), :] > 0, 0.0, MASKED)
                rows = pl.ds(g * ROWS + half * BLK, BLK)
                qx_ref[j, rows, HD:] = jnp.broadcast_to(bias, (BLK, HD)).astype(jnp.bfloat16)
    return lane, row


def attend_kernel(chunks, place_ref, qa_ref, qb_ref, mask_ref, *refs):
    kv_refs, (acc_out, top_out, den_out, qx_ref, kx_ref, vx_ref, s_ref, p_ref) = refs[:chunks], refs[chunks:]
    lane, row = load_operands(CHUNKS, place_ref, qa_ref, qb_ref, mask_ref, kv_refs, qx_ref, kx_ref, vx_ref)
    tops = {}
    for j in range(4):
        s_ref[j] = jnp.dot(qx_ref[j], kx_ref[...], preferred_element_type=jnp.float32)
    cols = pl.ds(pl.multiple_of(place_ref[0] * ROWS, ROWS), ROWS)
    for g in range(GROUP):
        rows = pl.ds(g * ROWS, ROWS)
        s_ref[0, rows, cols] = jnp.where(lane <= row, s_ref[0, rows, cols], MASKED)
    for j in range(4):
        for g in range(GROUP):
            rows = pl.ds(g * ROWS, ROWS)
            tops[j, g] = jnp.max(s_ref[j, rows, :], axis=1, keepdims=True)
    for j in range(4):
        for g in range(GROUP):
            rows = pl.ds(g * ROWS, ROWS)
            p_ref[j, rows, :] = jnp.exp2((s_ref[j, rows, :] - tops[j, g]) * SCALE2).astype(jnp.bfloat16)
    for j in range(4):
        both = jnp.dot(p_ref[j], vx_ref[...], preferred_element_type=jnp.float32)
        acc_out[j] = both[:, :HD]
        den_out[j] = both[:, HD:]
        for g in range(GROUP):
            top_out[j, pl.ds(g * ROWS, ROWS), :] = jnp.broadcast_to(tops[j, g], (ROWS, HD))


def attend_last_kernel(
    place_ref, qa_ref, qb_ref, mask_ref, kv_ref, acc_in, top_in, den_in, out_ref, qx_ref, kx_ref, vx_ref, s_ref
):
    base = CHUNKS + 3 * FAR
    lane, _ = load_operands(base, place_ref, qa_ref, qb_ref, mask_ref, [kv_ref], qx_ref, kx_ref, vx_ref)
    for j in range(4):
        s_ref[j] = jnp.dot(qx_ref[j], kx_ref[...], preferred_element_type=jnp.float32)
    for j in range(4):
        slot = j ^ place_ref[5]
        stats, tops, weights = [], [], []
        for g in range(GROUP):
            rows = pl.ds(g * ROWS, ROWS)
            scores = s_ref[j, rows, :]
            before = top_in[j, rows, :]
            highest = jnp.maximum(jnp.max(scores, axis=1, keepdims=True), before)
            shift = jnp.concatenate([highest] * (scores.shape[1] // HD), axis=1)
            weights.append(jnp.exp2((scores - shift) * SCALE2).astype(jnp.bfloat16))
            tops.append(highest)
        total = jnp.dot(jnp.concatenate(weights, axis=0), vx_ref[...], preferred_element_type=jnp.float32)
        for g in range(GROUP):
            rows = pl.ds(g * ROWS, ROWS)
            both, before, highest = total[g * ROWS : (g + 1) * ROWS], top_in[j, rows, :], tops[g]
            keep = jnp.exp2((before - highest) * SCALE2)
            acc = both[:, :HD] + keep * acc_in[j, rows, :]
            denominator = both[:, HD:] + keep * den_in[j, rows, :]
            out_ref[slot, rows, :] = (acc / denominator).astype(jnp.bfloat16)
            stats.append(highest * SCALE2 + jnp.log2(denominator))
        which = lane % GROUP
        level = jnp.where(which == 0, stats[0], jnp.where(which == 1, stats[1], stats[2]))
        high = level.astype(jnp.bfloat16).astype(jnp.float32)
        rest = level - high
        middle = rest.astype(jnp.bfloat16).astype(jnp.float32)
        parts = jnp.where(lane < GROUP, high, jnp.where(lane < 2 * GROUP, middle, rest - middle))
        out_ref[slot, pl.ds(QROWS, STAT), :] = parts.T[:STAT].astype(jnp.bfloat16)


def attend(place, qa, qb, masks, kvs, state=None):
    vmem = pl.BlockSpec(memory_space=pltpu.VMEM)
    keys = len(kvs) * FAR * ROWS
    scratch = [
        pltpu.VMEM((4, QROWS, 2 * HD), jnp.bfloat16),
        pltpu.VMEM((2 * HD, keys), jnp.bfloat16),
        pltpu.VMEM((keys, 2 * HD), jnp.bfloat16),
        pltpu.VMEM((4, QROWS, keys), jnp.float32),
    ]
    if state is None:
        kernel, name, state = functools.partial(attend_kernel, len(kvs)), "attend", ()
        outs = [jax.ShapeDtypeStruct((4, QROWS, HD), jnp.float32)] * 3
        scratch.append(pltpu.VMEM((4, QROWS, keys), jnp.bfloat16))
    else:
        kernel, name = attend_last_kernel, "attend_last"
        outs = jax.ShapeDtypeStruct((4, QROWS + STAT, HD), jnp.bfloat16)
    args = (place, qa, qb, masks, *kvs, *state)
    return pl.pallas_call(
        kernel,
        out_shape=outs,
        in_specs=[pl.BlockSpec(memory_space=pltpu.SMEM)] + [vmem] * (len(args) - 1),
        out_specs=[vmem] * 3 if isinstance(outs, list) else vmem,
        scratch_shapes=scratch,
        compiler_params=pltpu.CompilerParams(vmem_limit_bytes=32 * 2**20),
        name=name,
    )(*args)


def combine_kernel(p_ref, out_ref):
    parts = p_ref.shape[0]
    levels = []
    for i in range(parts):
        st = p_ref[i, pl.ds(QROWS, STAT), :].astype(jnp.float32)
        levels.append(st[0:GROUP] + st[GROUP : 2 * GROUP] + st[2 * GROUP : 3 * GROUP])
    top = levels[0]
    for i in range(1, parts):
        top = jnp.maximum(top, levels[i])
    shares = [jnp.exp2(level - top) for level in levels]
    total = shares[0]
    for i in range(1, parts):
        total = total + shares[i]
    shares = [share / total for share in shares]
    pad = jnp.zeros((HD - parts * GROUP, HD), jnp.float32)
    columns = jnp.concatenate(shares + [pad], axis=0).T
    for g in range(GROUP):
        acc = None
        for i in range(parts):
            c = i * GROUP + g
            term = p_ref[i, pl.ds(g * ROWS, ROWS), :].astype(jnp.float32) * columns[:, c : c + 1]
            acc = term if acc is None else acc + term
        out_ref[g] = acc.astype(jnp.bfloat16)


def combine(parts):
    vmem = pl.BlockSpec(memory_space=pltpu.VMEM)
    return pl.pallas_call(
        combine_kernel,
        out_shape=jax.ShapeDtypeStruct((GROUP, ROWS, HD), jnp.bfloat16),
        in_specs=[vmem],
        out_specs=vmem,
        compiler_params=pltpu.CompilerParams(vmem_limit_bytes=16 * 2**20),
        name="combine",
    )(parts)


def swap(value, axis):
    return lax.ppermute(value, axis, [(0, 1), (1, 0)])


def per_device(queries, key_states, value_states, head_masks):
    c, yh, zs, z0, ys, y0 = (lax.axis_index(a) for a in PLANE)
    y, z = yh * 4 + ys * 2 + y0, zs * 2 + z0

    kv = jnp.stack([key_states[0, 0], value_states[0, 0]])
    kv = kv.transpose(2, 0, 1, 3).reshape(4, 2, 2, 16, HD)
    even, odd = kv[:, 0], kv[:, 1]
    give = jnp.where(c == 0, odd, even)
    got = swap(give, "c")
    low = jnp.where(c == 0, even, got)
    high = jnp.where(c == 0, got, odd)
    kv = jnp.stack([low, high], axis=1)
    kv = jnp.broadcast_to(kv[:, None], (4, FAR, 2, 2, 16, HD)).reshape(4 * FAR, 2, 2, 16, HD)
    own = lax.all_to_all(kv, AXES, 0, 0, axis_index_groups=first_axis_groups(), tiled=True)

    mine = queries.transpose(1, 0, 2)
    qa = jnp.stack([mine, swap(mine, "y0")])
    qb = swap(qa, "z0")

    low = lax.ppermute(own, PLANE, second_axis_xor(6))
    high = lax.ppermute(own, PLANE, second_axis_xor(2))
    far = lax.ppermute(low, PLANE, second_axis_xor(2, relay=True))
    own, low, high, far = (a.reshape(4, FAR, 2, 2, 16, HD) for a in (own, low, high, far))

    q_shards = [shard_of(y ^ (j & 1), z ^ (j >> 1)) for j in range(4)]
    k_shards = []
    for bits in (0, 2, 6, 4):
        for k in range(FAR):
            yk = jnp.where(c == 0, y ^ bits, 2 * k + y0)
            zk = jnp.where(c == 0, 2 * k + z0, z ^ bits)
            k_shards.append(shard_of(yk, zk))
    own_place = jnp.where(c == 0, z >> 1, y >> 1)
    me = z0 * 2 + y0
    zero = jnp.int32(0)
    place = jnp.stack([own_place, *q_shards, me, zero, zero, *k_shards]).astype(jnp.int32)

    state = attend(place, qa, qb, head_masks, [own, high, low])
    parts = attend(place, qa, qb, head_masks, [far], state)
    parts = lax.all_to_all(parts, BLOCK, 0, 0, tiled=True)
    return combine(parts).transpose(1, 0, 2)


def solution(mesh):
    fine = Mesh(mesh.devices.reshape(SIZES), AXES)
    return jax.shard_map(
        per_device,
        mesh=fine,
        in_specs=(P(TOK, HEAD, None), P(TOK, HEAD), P(TOK, HEAD), P(HEAD)),
        out_specs=P(TOK, HEAD, None),
        check_vma=False,
    )
```
